256 devices in a mesh: seq: 128 (over z_lo, x, y, core), ch: 2 (over z_hi).
Axes of the slice: x: 4, y: 4, z: 8 (z_hi: 2, z_lo: 4; z = z_hi * 4 + z_lo), core: 2. Of those that a mesh axis runs over, the one named last changes fastest.
Arguments:
- query_branch: bfloat16 [16384, 1024], P('seq', 'ch'), may hold values from -6 to 6
- key_branch: bfloat16 [16384, 1024], P('seq', 'ch'), may hold values from -44.5 to 44.5, as said below
- value_branch: bfloat16 [16384, 1024], P('seq', 'ch'), may hold values from -44.5 to 44.5, as said below
- filter_taps: float32 [16384, 1024], P('seq', 'ch'), may hold values from -1.5 to 1.5, as said below
- skip_gain: float32 [1024], P('ch'), may hold values from -2.8 to 2.8, as said below
- out_weight: bfloat16 [1024, 8192], P('ch'), may hold values from -0.1875 to 0.1875
Outputs:
- mixed: bfloat16 [16384, 8192], P('seq')
The draws below stay inside these ranges and needn't reach their ends.
Inputs may be any that keep to these rules, and one draw needn't show every extreme that they name: `filter_taps`: real filter taps, one column a channel. `key_branch`: real values. `value_branch`: real values. `skip_gain`: one real number a channel.
All inputs are finite; a program needn't handle non-finite values.
Results may differ from the reference program's by a relative error of at most 0.0049.
Values may be sent and summed in bfloat16 or wider, within the bound.
A program may use at most 128 MiB of HBM per device.

```python
import math
import jax
import jax.numpy as jnp

D = 8192
CHANNELS = 1024
SEQ_LEN = 16384


def channel_gain(key):
    gain_key = jax.random.fold_in(key, 101)
    return jnp.exp(jax.random.uniform(gain_key, (CHANNELS,), jnp.float32, -4.0, 0.0))


def envelope_scale(rates):
    return jnp.sqrt(2.0 * rates / -jnp.expm1(-2.0 * rates * SEQ_LEN))


def branch_values(key, salt):
    gains = channel_gain(key)
    key = jax.random.fold_in(key, salt)
    noise = jnp.clip(jax.random.normal(key, (SEQ_LEN, CHANNELS), jnp.float32), -6.0, 6.0)
    return (noise * jax.lax.rsqrt(gains)[None, :]).astype(jnp.bfloat16)


def draw_key_branch(key, part):
    return branch_values(key, 11)


def draw_value_branch(key, part):
    return branch_values(key, 13)


def draw_skip_gain(key, part):
    gains = channel_gain(key)
    key = jax.random.fold_in(key, 17)
    noise = jnp.clip(jax.random.normal(key, (CHANNELS,), jnp.float32), -4.0, 4.0)
    return (0.7 * noise * gains).astype(jnp.float32)


def draw_filter_taps(key, part):
    gains = channel_gain(key)
    key = jax.random.fold_in(key, 7)
    rate_key, slow_key, share_key, noise_key = jax.random.split(key, 4)
    tap_index = jnp.arange(SEQ_LEN, dtype=jnp.float32)[:, None]
    slow_low = math.log(1.0 / (8.0 * SEQ_LEN))
    slow_high = math.log(1.0 / (2.0 * SEQ_LEN))
    slow_rates = jnp.exp(jax.random.uniform(slow_key, (CHANNELS,), jnp.float32, slow_low, slow_high))
    slow_share = jax.random.uniform(share_key, (CHANNELS,), jnp.float32, 0.25, 0.5)
    rate_low = math.log(1.0 / (2.0 * SEQ_LEN))
    rate_high = math.log(1.0 / 30.0)
    decay_rates = jnp.exp(jax.random.uniform(rate_key, (CHANNELS,), jnp.float32, rate_low, rate_high))
    raw_taps = jnp.clip(jax.random.normal(noise_key, (SEQ_LEN, CHANNELS), jnp.float32), -5.0, 5.0)
    fast_part = jnp.exp(-decay_rates[None, :] * tap_index) * envelope_scale(decay_rates)[None, :]
    slow_part = jnp.exp(-slow_rates[None, :] * tap_index) * envelope_scale(slow_rates)[None, :]
    envelope = jnp.sqrt(1.0 - slow_share)[None, :] * fast_part + jnp.sqrt(slow_share)[None, :] * slow_part
    return (raw_taps * envelope * gains[None, :]).astype(jnp.float32)


def levels(key, shape, cuts, smallest, high):
    factor_of, own = 1.0, jax.random.fold_in(key, 6)
    for axis_at, parts in cuts:
        steps = jnp.exp(jax.random.uniform(jax.random.fold_in(own, axis_at), (parts,), jnp.float32, smallest / len(cuts), high / len(cuts)))
        factor_of = factor_of * jnp.repeat(steps, shape[axis_at] // parts).reshape([-1 if axis == axis_at else 1 for axis in range(len(shape))])
    return factor_of


def centred(own_key, dims, scale, bound, pieces=(), kind=jnp.bfloat16):
    loudness = levels(own_key, dims, pieces, -0.22, 0.18) if pieces else 1.0
    result = jax.random.normal(own_key, dims, jnp.float32) * scale * loudness
    return jnp.minimum(jnp.maximum(result, -bound), bound).astype(kind)


def setup_inputs(seed: int = 0) -> dict:
    arg_keys = jax.random.split(jax.random.key(seed), 7)
    return {
        "query_branch": centred(arg_keys[0], (SEQ_LEN, CHANNELS), 1.0, 6.0, ((0, 128), (1, 2))),
        "key_branch": draw_key_branch(jax.random.fold_in(arg_keys[6], 71), 0),
        "value_branch": draw_value_branch(jax.random.fold_in(arg_keys[6], 71), 0),
        "filter_taps": draw_filter_taps(jax.random.fold_in(arg_keys[6], 71), 0),
        "skip_gain": draw_skip_gain(jax.random.fold_in(arg_keys[6], 71), 0),
        "out_weight": centred(arg_keys[5], (CHANNELS, D), CHANNELS ** -0.5, 0.1875, ((0, 2),)),
    }


def reference(query_branch, key_branch, value_branch, filter_taps, skip_gain, out_weight):
    product = key_branch.astype(jnp.float32) * value_branch.astype(jnp.float32)
    spec_input = jnp.fft.rfft(product, n=2 * SEQ_LEN, axis=0)
    spec_filter = jnp.fft.rfft(filter_taps, n=2 * SEQ_LEN, axis=0)
    convolved = jnp.fft.irfft(spec_input * spec_filter, n=2 * SEQ_LEN, axis=0)[:SEQ_LEN]
    gated_values = (query_branch.astype(jnp.float32) * (convolved + skip_gain[None, :] * product)).astype(jnp.bfloat16)
    return jnp.dot(gated_values, out_weight, preferred_element_type=jnp.float32).astype(jnp.bfloat16)
```

```python
import math

import jax
import jax.numpy as jnp
import numpy as np
from jax import lax
from jax.sharding import PartitionSpec as P

bf16 = jnp.bfloat16
f32 = jnp.float32


def tables(blocks, span):
    alpha = np.arange(blocks)[:, None] + 0.5
    fine = np.arange(span)
    ahead = 2.0 * np.pi * alpha * np.arange(blocks)[None, :] / (2 * blocks)
    turn = 2.0 * np.pi * alpha * fine[None, :] / (2 * blocks * span)
    inner = 2.0 * np.pi * (fine[:, None] * fine[None, :] % span) / span
    first = np.concatenate([np.cos(ahead), -np.sin(ahead)], 0)
    second = np.block([[np.cos(inner), -np.sin(inner)], [np.sin(inner), np.cos(inner)]])
    back = np.block([[np.cos(inner), np.sin(inner)], [-np.sin(inner), np.cos(inner)]])
    last = np.concatenate([np.cos(ahead), -np.sin(ahead)], 0).T / (blocks * span)
    as32 = lambda t: jnp.asarray(t.astype(np.float32))
    return as32(first), as32(np.cos(turn)), as32(-np.sin(turn)), as32(second), as32(back), as32(last)


def mm(form, a, b):
    return jnp.einsum(form, a, b, precision=lax.Precision.HIGH, preferred_element_type=f32)


def body(query_branch, key_branch, value_branch, filter_taps, skip_gain, out_weight):
    span, width = key_branch.shape
    n_seq = lax.axis_size("seq")
    n_ch = lax.axis_size("ch")
    me = lax.axis_index("seq")
    rows = width // n_seq
    mine = lax.dynamic_slice_in_dim(out_weight, me * rows, rows, 0)
    theirs = lax.ppermute(mine, "ch", [(i, i ^ 1) for i in range(n_ch)])
    other_weight = lax.all_gather(theirs, "seq", tiled=True)

    product = key_branch.astype(f32) * value_branch.astype(f32)
    pair = jnp.stack([product.T, filter_taps.T]).astype(bf16)
    pair = pair.reshape(2, n_seq, rows, span).transpose(1, 0, 2, 3)
    got = lax.all_to_all(pair, "seq", 0, 0)
    first, tw_re, tw_im, second, back, last = tables(n_seq, span)
    x = mm("ka,ascb->sckb", first.astype(f32), got.astype(f32))
    re, im = x[:, :, :n_seq], x[:, :, n_seq:]
    x = jnp.concatenate([re * tw_re - im * tw_im, re * tw_im + im * tw_re], -1)
    x = mm("sckb,bj->sckj", x, second)
    re, im = x[..., :span], x[..., span:]
    z = jnp.concatenate([re[0] * re[1] - im[0] * im[1], re[0] * im[1] + im[0] * re[1]], -1)
    z = mm("ckj,jb->ckb", z, back)
    re, im = z[..., :span], z[..., span:]
    z = jnp.concatenate([re * tw_re + im * tw_im, im * tw_re - re * tw_im], 1)
    y = mm("ak,ckb->acb", last, z)
    conv = lax.all_to_all(y.astype(bf16), "seq", 0, 0)
    convolved = conv.reshape(width, span).T.astype(f32)
    gated = (query_branch.astype(f32) * (convolved + skip_gain[None, :] * product)).astype(bf16)
    gated_other = lax.ppermute(gated, "ch", [(i, i ^ 1) for i in range(n_ch)])
    mixed = jnp.dot(gated, out_weight, preferred_element_type=f32)
    mixed = mixed + jnp.dot(gated_other, other_weight, preferred_element_type=f32)
    return mixed.astype(bf16)


def solution(mesh):
    return jax.shard_map(
        body,
        mesh=mesh,
        in_specs=(P("seq", "ch"), P("seq", "ch"), P("seq", "ch"), P("seq", "ch"), P("ch"), P("ch", None)),
        out_specs=P("seq", None),
        check_vma=False,
    )
```

```python
import functools
import math

import jax
import jax.numpy as jnp
import numpy as np
from jax import lax
from jax.experimental import pallas as pl
from jax.experimental.pallas import tpu as pltpu
from jax.sharding import PartitionSpec as P

bf16 = jnp.bfloat16
f32 = jnp.float32
MESH = pl.DeviceIdType.MESH
SPAN = 128
BLOCKS = 128
CH = 4
TILE = 512
QUARTER = 2048


def split(t):
    hi = t.astype(bf16)
    return hi, (t - hi.astype(f32)).astype(bf16)


def tables():
    n = 2 * BLOCKS
    at = np.arange(BLOCKS)
    a = (at % 8) // 2 * 32 + at // 8 * 2 + at % 2
    alpha = np.arange(BLOCKS)[:, None] + 0.5
    fine = np.arange(SPAN)
    ahead = 2.0 * np.pi * alpha * a[None, :] / n
    turn = 2.0 * np.pi * alpha * fine[None, :] / (n * SPAN)
    inner = 2.0 * np.pi * (fine[:, None] * fine[None, :] % SPAN) / SPAN
    first = np.concatenate([np.cos(ahead), -np.sin(ahead)], 0)
    second = np.block([[np.cos(inner), -np.sin(inner)], [np.sin(inner), np.cos(inner)]])
    back = np.block([[np.cos(inner), np.sin(inner)], [-np.sin(inner), np.cos(inner)]])
    last = first.T / (BLOCKS * SPAN)

    def parts(t):
        hi = t.astype(jnp.bfloat16)
        return hi, (t - hi.astype(np.float64)).astype(jnp.bfloat16)

    fh, fl = parts(first)
    sh, sl = parts(second)
    bh, bl = parts(back)
    lh, ll = parts(last)
    return (
        jnp.asarray(np.concatenate([fh, fl], 1)),
        jnp.asarray(np.concatenate([sh, sh, sl], 0)),
        jnp.asarray(np.concatenate([bh, bh, bl], 0)),
        jnp.asarray(np.concatenate([lh, lh, ll], 1)),
        jnp.asarray(np.stack([np.cos(turn), -np.sin(turn)]).astype(np.float32)),
    )


def kernel(
    q_ref, k_ref, v_ref, taps_ref, skip_ref, t1_ref, t2_ref, t3_ref, t4_ref, tw_ref, w_ref, out_ref,
    s1, r1, r2, s1q, r1q, r2q, s3, r3, r4, wown, wo, acc, rows8, rows4, xcat, lhs2, lhs3, rhs4,
    own_sem, p1_s, p1_r, p1q_s, p1q_r, p2_s, p2_r, p2q_s, p2q_r, p3_s, p3_r, p4_s, p4_r,
    seed_s, seed_r, st1_s, st1_r, st2_s, st2_r, d2d_s, d2d_r,
):
    me = lax.axis_index("seq")
    g = lax.axis_index("ch")
    z, xy, k = me // 32, me // 2 % 16, me % 2
    x, y = xy // 4, xy % 4
    zk = z * 2 + k

    def dev(z_, xy_, k_, g_):
        return (z_ * 32 + xy_ * 2 + k_, g_)

    def remote(src, dst, ss, rs, to):
        return pltpu.make_async_remote_copy(
            src_ref=src, dst_ref=dst, send_sem=ss, recv_sem=rs, device_id=to, device_id_type=MESH
        )

    barrier = pltpu.get_barrier_semaphore()

    @pl.loop(1, 16)
    def _(i):
        pl.semaphore_signal(barrier, inc=1, device_id=dev(z, (xy + i) % 16, k, g), device_id_type=MESH)

    @pl.loop(1, 8)
    def _(i):
        to = (zk + i) % 8
        pl.semaphore_signal(barrier, inc=1, device_id=dev(to // 2, xy, to % 2, g), device_id_type=MESH)

    @pl.loop(0, 8)
    def _(i):
        pl.semaphore_signal(barrier, inc=1, device_id=dev(i // 2, xy, i % 2, 1 - g), device_id_type=MESH)

    own = pltpu.make_async_copy(w_ref, wown, own_sem)
    own.start()

    ut = (k_ref[...].astype(f32) * v_ref[...].astype(f32)).T
    ht = taps_ref[...].T
    both = jnp.concatenate([ut.reshape(BLOCKS, CH, SPAN), ht.reshape(BLOCKS, CH, SPAN)], 1).astype(bf16)
    both = both.reshape(4, 16, 2, 2 * CH, SPAN)
    for i in range(8):
        s1[i] = both[i // 2, :, i % 2]

    pl.semaphore_wait(barrier, 30)

    def p1(i, src, dst, ss, rs):
        to = (zk + i) % 8
        return remote(src.at[to], dst.at[zk], ss.at[to], rs.at[zk], dev(to // 2, xy, to % 2, g))

    def p1_from(i, src, dst, ss, rs):
        fr = (zk + 8 - i) % 8
        return remote(src.at[fr], dst.at[fr], ss.at[fr], rs.at[fr], dev(fr // 2, xy, fr % 2, g))

    def p2(i, src, dst, ss, rs):
        to = (xy + i) % 16
        return remote(src.at[:, to], dst.at[xy], ss.at[to], rs.at[xy], dev(z, to, k, g))

    def p2_from(i, src, dst, ss, rs):
        fr = (xy + 16 - i) % 16
        return remote(src.at[:, fr], dst.at[fr], ss.at[fr], rs.at[fr], dev(z, fr, k, g))

    def p3(i):
        to = (xy + i) % 16
        return remote(s3.at[to], r3.at[xy], p3_s.at[to], p3_r.at[xy], dev(z, to, k, g))

    def p3_from(i):
        fr = (xy + 16 - i) % 16
        return remote(s3.at[fr], r3.at[fr], p3_s.at[fr], p3_r.at[fr], dev(z, fr, k, g))

    def p4(i, group):
        to = (zk + i) % 8
        return remote(
            r3.at[:, to], r4.at[g, z, :, k], p4_s.at[group, to], p4_r.at[g, zk], dev(to // 2, xy, to % 2, group)
        )

    def p4_from(i, group):
        fr = (zk + 8 - i) % 8
        return remote(
            r3.at[:, fr], r4.at[group, fr // 2, :, fr % 2], p4_s.at[group, fr], p4_r.at[group, fr],
            dev(fr // 2, xy, fr % 2, group),
        )

    def uv(h):
        return (x, y) if h == 0 else (y, x)

    def place(h, u, v):
        return u % 4 * 4 + v % 4 if h == 0 else v % 4 * 4 + u % 4

    def block(h, sub, at):
        return wo.at[h, sub, k * 16 + at]

    def seed(h, sub, from_own):
        zn = (g * 4 + z + 7 + 2 * h) % 8
        src = w_ref.at[
            pl.ds(pl.multiple_of((k * 16 + xy) * 16, 16), 16), pl.ds(pl.multiple_of((h * 2 + sub) * QUARTER, QUARTER), QUARTER)
        ] if from_own else block(h, sub, xy)
        return remote(src, block(h, sub, xy), seed_s.at[h, sub], seed_r.at[h, sub], dev(zn % 4, xy, k, zn // 4))

    def st1(h, side, sub, off=0):
        u, v = uv(h)
        at = place(h, u + off + 4, v)
        slot = 0 if off == 0 else 1
        to = place(h, u + (1 if side == 0 else 3), v)
        return remote(
            block(h, sub, at), block(h, sub, at), st1_s.at[h, slot, side, sub], st1_r.at[h, slot, side, sub], dev(z, to, k, g)
        )

    def st2(h, e, side, sub, off=0):
        u, v = uv(h)
        at = place(h, u + e + 4, v + off + 4)
        slot = 0 if off == 0 else 1
        to = place(h, u, v + (1 if side == 0 else 3))
        return remote(
            block(h, sub, at), block(h, sub, at), st2_s.at[h, e % 4, slot, side, sub], st2_r.at[h, e % 4, slot, side, sub],
            dev(z, to, k, g),
        )

    def d2d(h, at, core):
        return remote(
            wo.at[h, :, core * 16 + at], wo.at[h, :, core * 16 + at], d2d_s.at[h, at], d2d_r.at[h, at], dev(z, xy, 1 - k, g)
        )

    def spread(h, e, sub):
        for side in (0, 1):
            st2(h, e, side, sub).start()

    def seed_step_of(h, sub):
        seed(h, sub, False).wait_recv()

        @pl.when(z != 3 * h)
        def _():
            seed(h, sub, False).start()

        for side in (0, 1):
            st1(h, side, sub).start()
        spread(h, 0, sub)
        if sub == 1:
            d2d(h, xy, k).start()

    def seed_steps(first):
        for h in (0, 1):

            @pl.when((z >= 2) == ((h == 0) == first))
            def _():
                for sub in (0, 1):
                    seed_step_of(h, sub)

    def ring1(h):
        u, v = uv(h)
        for sub in (0, 1):
            st1(h, 0, sub).wait_recv()
            if sub == 0:
                st1(h, 0, 0, -1).start()
            st1(h, 1, sub).wait_recv()
            if sub == 1:
                st1(h, 1, 1, 1).start()
            spread(h, -1, sub)
            spread(h, 1, sub)
        d2d(h, place(h, u + 3, v), k).start()
        d2d(h, place(h, u + 1, v), k).start()

    def ring1_far(h):
        u, v = uv(h)
        st1(h, 0, 0, -1).wait_recv()
        spread(h, 2, 0)
        st1(h, 1, 1, 1).wait_recv()
        spread(h, 2, 1)
        d2d(h, place(h, u + 2, v), k).start()

    def ring2(h, e):
        u, v = uv(h)
        for sub in (0, 1):
            st2(h, e, 0, sub).wait_recv()
            if sub == 0:
                st2(h, e, 0, 0, -1).start()
            st2(h, e, 1, sub).wait_recv()
            if sub == 1:
                st2(h, e, 1, 1, 1).start()
        d2d(h, place(h, u + e + 4, v + 3), k).start()
        d2d(h, place(h, u + e + 4, v + 1), k).start()

    def ring2_far(h, e):
        u, v = uv(h)
        st2(h, e, 0, 0, -1).wait_recv()
        st2(h, e, 1, 1, 1).wait_recv()
        d2d(h, place(h, u + e + 4, v + 2), k).start()

    @pl.loop(1, 8)
    def _(i):
        p1(i, s1, r1, p1_s, p1_r).start()

    for h in (0, 1):

        @pl.when(z == 3 * h)
        def _():
            for sub in (0, 1):
                seed(h, sub, True).start()

    qt = q_ref[...].astype(f32).T.reshape(BLOCKS, CH, SPAN).astype(bf16).reshape(4, 16, 2, CH, SPAN)
    for i in range(8):
        s1q[i] = qt[i // 2, :, i % 2]

    @pl.loop(1, 8)
    def _(i):
        p1(i, s1q, r1q, p1q_s, p1q_r).start()

    r1[zk] = s1[zk]
    r1q[zk] = s1q[zk]

    seed_steps(True)

    @pl.loop(1, 8)
    def _(i):
        p1_from(i, s1, r1, p1_s, p1_r).wait_recv()

    @pl.loop(1, 16)
    def _(i):
        p2(i, r1, r2, p2_s, p2_r).start()

    r2[xy] = r1[:, xy]

    @pl.loop(1, 8)
    def _(i):
        p1_from(i, s1q, r1q, p1q_s, p1q_r).wait_recv()

    @pl.loop(1, 16)
    def _(i):
        p2(i, r1q, r2q, p2q_s, p2q_r).start()

    r2q[xy] = r1q[:, xy]

    seed_steps(False)

    @pl.loop(1, 16)
    def _(i):
        p2_from(i, r1, r2, p2_s, p2_r).wait_recv()

    rows8[...] = r2[...].reshape(BLOCKS, 2 * CH, SPAN).astype(f32).reshape(BLOCKS * 2 * CH, SPAN)
    for r in range(2 * CH):
        part = rows8[pl.ds(r, BLOCKS, stride=2 * CH), :].astype(bf16)
        xcat[0:BLOCKS, r * SPAN : (r + 1) * SPAN] = part
        xcat[BLOCKS : 2 * BLOCKS, r * SPAN : (r + 1) * SPAN] = part
    for r in range(2 * CH):
        got = jnp.dot(t1_ref[...], xcat[:, r * SPAN : (r + 1) * SPAN], preferred_element_type=f32)
        re, im = got[:BLOCKS], got[BLOCKS:]
        hi, lo = split(jnp.concatenate([re * tw_ref[0] - im * tw_ref[1], re * tw_ref[1] + im * tw_ref[0]], 1))
        lhs2[r * BLOCKS : (r + 1) * BLOCKS, 0:256] = hi
        lhs2[r * BLOCKS : (r + 1) * BLOCKS, 256:512] = lo
        lhs2[r * BLOCKS : (r + 1) * BLOCKS, 512:768] = hi

    ring1(0)
    ring1(1)

    for c in range(CH):
        rows = pl.ds(c * BLOCKS, BLOCKS)
        left = jnp.dot(lhs2[rows, :], t2_ref[...], preferred_element_type=f32)
        right = jnp.dot(lhs2[pl.ds((c + CH) * BLOCKS, BLOCKS), :], t2_ref[...], preferred_element_type=f32)
        lr, li, rr, ri = left[:, :SPAN], left[:, SPAN:], right[:, :SPAN], right[:, SPAN:]
        hi, lo = split(jnp.concatenate([lr * rr - li * ri, lr * ri + li * rr], 1))
        lhs3[rows, 0:256] = hi
        lhs3[rows, 256:512] = lo
        lhs3[rows, 512:768] = hi

    ring1_far(0)
    ring1_far(1)

    for c in range(CH):
        rows = pl.ds(c * BLOCKS, BLOCKS)
        got = jnp.dot(lhs3[rows, :], t3_ref[...], preferred_element_type=f32)
        re, im = got[:, :SPAN], got[:, SPAN:]
        cols = pl.ds(c * SPAN, SPAN)
        hi, lo = split(jnp.concatenate([re * tw_ref[0] + im * tw_ref[1], im * tw_ref[0] - re * tw_ref[1]], 0))
        rhs4[0:256, cols] = hi
        rhs4[256:512, cols] = lo
        rhs4[512:768, cols] = hi

    @pl.loop(1, 16)
    def _(i):
        p2_from(i, r1q, r2q, p2q_s, p2q_r).wait_recv()

    rows4[...] = r2q[...].reshape(BLOCKS, CH, SPAN).astype(f32).reshape(BLOCKS * CH, SPAN)
    for c in range(CH):
        conv = jnp.dot(t4_ref[...], rhs4[:, c * SPAN : (c + 1) * SPAN], preferred_element_type=f32)
        at = pl.ds(c, BLOCKS, stride=CH)
        signal = rows8[pl.ds(c, BLOCKS, stride=2 * CH), :]
        rows4[at, :] = rows4[at, :] * (conv + skip_ref[0, me * CH + c] * signal)
    s3[...] = rows4[...].astype(bf16).reshape(16, 8, CH, SPAN)

    @pl.loop(1, 16)
    def _(i):
        p3(i).start()

    r3[xy] = s3[xy]

    ring2(0, 0)
    ring2(1, 0)

    @pl.loop(1, 16)
    def _(i):
        p3_from(i).wait_recv()

    @pl.loop(0, 8)
    def _(i):
        p4(i, 1 - g).start()

    @pl.loop(1, 8)
    def _(i):
        p4(i, g).start()

    r4[g, z, :, k] = r3[:, zk]

    for e in (-1, 1):
        for h in (0, 1):
            ring2(h, e)

    @pl.loop(1, 8)
    def _(i):
        p4_from(i, g).wait_recv()

    own.wait()
    here = r4[g].reshape(512, SPAN).T

    @pl.loop(0, 8)
    def _(t):
        cols = pl.ds(pl.multiple_of(t * TILE, TILE), TILE)
        acc[:, cols] = jnp.dot(here, wown[:, cols], preferred_element_type=f32)

    for h in (0, 1):
        ring2(h, 2)
    for e in (0, -1, 1):
        for h in (0, 1):
            ring2_far(h, e)

    @pl.loop(8, 16)
    def _(t):
        cols = pl.ds(pl.multiple_of(t * TILE, TILE), TILE)
        acc[:, cols] = jnp.dot(here, wown[:, cols], preferred_element_type=f32)

    for h in (0, 1):
        ring2_far(h, 2)

    @pl.loop(0, 8)
    def _(i):
        p4_from(i, 1 - g).wait_recv()

    there = r4[1 - g].reshape(512, SPAN).T

    @pl.loop(0, 16)
    def _(i):
        d2d(0, i, 1 - k).wait_recv()
        d2d(1, i, 1 - k).wait_recv()

    for part in range(4):
        for t in range(QUARTER // TILE):
            base = part * QUARTER + t * TILE
            weight = wo[part // 2, part % 2, :, :, t * TILE : (t + 1) * TILE].reshape(512, TILE)
            total = acc[:, base : base + TILE] + jnp.dot(there, weight, preferred_element_type=f32)
            out_ref[:, base : base + TILE] = total.astype(bf16)

    @pl.loop(1, 8)
    def _(i):
        p1(i, s1, r1, p1_s, p1_r).wait_send()
        p1(i, s1q, r1q, p1q_s, p1q_r).wait_send()
        p4(i, g).wait_send()

    @pl.loop(1, 16)
    def _(i):
        p2(i, r1, r2, p2_s, p2_r).wait_send()
        p2(i, r1q, r2q, p2q_s, p2q_r).wait_send()
        p3(i).wait_send()

    @pl.loop(0, 8)
    def _(i):
        p4(i, 1 - g).wait_send()

    @pl.loop(0, 16)
    def _(i):
        d2d(0, i, k).wait_send()
        d2d(1, i, k).wait_send()

    for h in (0, 1):
        for sub in (0, 1):
            seed(h, sub, False).wait_send()
            for side in (0, 1):
                st1(h, side, sub).wait_send()
                for e in (0, -1, 1, 2):
                    st2(h, e, side, sub).wait_send()
        st1(h, 0, 0, -1).wait_send()
        st1(h, 1, 1, 1).wait_send()
        for e in (0, -1, 1, 2):
            st2(h, e, 0, 0, -1).wait_send()
            st2(h, e, 1, 1, 1).wait_send()


def body(query_branch, key_branch, value_branch, filter_taps, skip_gain, out_weight):
    width = out_weight.shape[1]
    vmem, hbm = pl.BlockSpec(memory_space=pltpu.VMEM), pl.BlockSpec(memory_space=pl.ANY)
    dma = pltpu.SemaphoreType.DMA
    v = pltpu.VMEM
    return pl.pallas_call(
        kernel,
        out_shape=jax.ShapeDtypeStruct((SPAN, width), bf16),
        in_specs=[vmem] * 4 + [pl.BlockSpec(memory_space=pltpu.SMEM)] + [vmem] * 5 + [hbm],
        out_specs=vmem,
        scratch_shapes=[
            v((8, 16, 2 * CH, SPAN), bf16), v((8, 16, 2 * CH, SPAN), bf16), v((16, 8, 2 * CH, SPAN), bf16),
            v((8, 16, CH, SPAN), bf16), v((8, 16, CH, SPAN), bf16), v((16, 8, CH, SPAN), bf16),
            v((16, 8, CH, SPAN), bf16), v((16, 8, CH, SPAN), bf16), v((2, 4, 16, 2, CH, SPAN), bf16),
            v((512, width), bf16), v((2, 2, 32, 16, QUARTER), bf16), v((SPAN, width), f32),
            v((BLOCKS * 2 * CH, SPAN), f32), v((BLOCKS * CH, SPAN), f32),
            v((256, 2 * CH * SPAN), bf16), v((2 * CH * BLOCKS, 768), bf16), v((CH * BLOCKS, 768), bf16), v((768, CH * SPAN), bf16),
            dma, dma((8,)), dma((8,)), dma((8,)), dma((8,)), dma((16,)), dma((16,)), dma((16,)), dma((16,)),
            dma((16,)), dma((16,)), dma((2, 8)), dma((2, 8)),
            dma((2, 2)), dma((2, 2)), dma((2, 2, 2, 2)), dma((2, 2, 2, 2)), dma((2, 4, 2, 2, 2)), dma((2, 4, 2, 2, 2)),
            dma((2, 16)), dma((2, 16)),
        ],
        compiler_params=pltpu.CompilerParams(collective_id=0, has_side_effects=True, vmem_limit_bytes=56 * 2**20),
    )(query_branch, key_branch, value_branch, filter_taps, skip_gain.reshape(1, -1), *tables(), out_weight)


def solution(mesh):
    return jax.shard_map(
        body,
        mesh=mesh,
        in_specs=(P("seq", "ch"), P("seq", "ch"), P("seq", "ch"), P("seq", "ch"), P("ch"), P("ch", None)),
        out_specs=P("seq", None),
        check_vma=False,
    )
```

```python
import functools
import math

import jax
import jax.numpy as jnp
import numpy as np
from jax import lax
from jax.experimental import pallas as pl
from jax.experimental.pallas import tpu as pltpu
from jax.sharding import PartitionSpec as P

bf16 = jnp.bfloat16
f32 = jnp.float32
MESH = pl.DeviceIdType.MESH
SPAN = 128
BLOCKS = 128
CH = 4
TILE = 512
QUARTER = 2048


def split(t):
    hi = t.astype(bf16)
    return hi, (t - hi.astype(f32)).astype(bf16)


def tables():
    n = 2 * BLOCKS
    at = np.arange(BLOCKS)
    a = (at % 8) // 2 * 32 + at // 8 * 2 + at % 2
    alpha = np.arange(BLOCKS)[:, None] + 0.5
    fine = np.arange(SPAN)
    ahead = 2.0 * np.pi * alpha * a[None, :] / n
    turn = 2.0 * np.pi * alpha * fine[None, :] / (n * SPAN)
    inner = 2.0 * np.pi * (fine[:, None] * fine[None, :] % SPAN) / SPAN
    first = np.concatenate([np.cos(ahead), -np.sin(ahead)], 0)
    second = np.block([[np.cos(inner), -np.sin(inner)], [np.sin(inner), np.cos(inner)]])
    back = np.block([[np.cos(inner), np.sin(inner)], [-np.sin(inner), np.cos(inner)]])
    last = first.T / (BLOCKS * SPAN)

    as32 = lambda t: jnp.asarray(t.astype(np.float32))
    return as32(first), as32(second), as32(back), as32(last), as32(np.stack([np.cos(turn), -np.sin(turn)]))


def kernel(
    q_hbm, k_hbm, v_hbm, taps_hbm, skip_ref, t1_hbm, t2_hbm, t3_hbm, t4_hbm, tw_hbm, w_ref, out_ref,
    q_ref, k_ref, v_ref, taps_ref, t1_raw, t2_raw, t3_raw, t4_raw, tw_ref, load_sem, t1_ref, t2_ref, t3_ref, t4_ref,
    s1, r1, r2, s1q, r1q, r2q, s3, r3, r4, wown, wo, acc, rows8, rows4, xcat, lhs2, lhs3, rhs4,
    own_sem, p1_s, p1_r, p1q_s, p1q_r, p2_s, p2_r, p2q_s, p2q_r, p3_s, p3_r, p4_s, p4_r,
    fresh_s, seed_r, st1_s, st1_r, st2_s, st2_r, d2d_s, d2d_r, result, out_sem,
):
    me = lax.axis_index("seq")
    g = lax.axis_index("ch")
    z, xy, k = me // 32, me // 2 % 16, me % 2
    x, y = xy // 4, xy % 4
    zk = z * 2 + k

    def dev(z_, xy_, k_, g_):
        return (z_ * 32 + xy_ * 2 + k_, g_)

    def remote(src, dst, ss, rs, to):
        return pltpu.make_async_remote_copy(
            src_ref=src, dst_ref=dst, send_sem=ss, recv_sem=rs, device_id=to, device_id_type=MESH
        )

    barrier = pltpu.get_barrier_semaphore()

    @pl.loop(1, 16)
    def _(i):
        pl.semaphore_signal(barrier, inc=1, device_id=dev(z, (xy + i) % 16, k, g), device_id_type=MESH)

    @pl.loop(1, 8)
    def _(i):
        to = (zk + i) % 8
        pl.semaphore_signal(barrier, inc=1, device_id=dev(to // 2, xy, to % 2, g), device_id_type=MESH)

    @pl.loop(0, 8)
    def _(i):
        pl.semaphore_signal(barrier, inc=1, device_id=dev(i // 2, xy, i % 2, 1 - g), device_id_type=MESH)

    loads = [
        pltpu.make_async_copy(src, dst, load_sem.at[i])
        for i, (src, dst) in enumerate([
            (k_hbm, k_ref), (v_hbm, v_ref), (taps_hbm, taps_ref), (q_hbm, q_ref),
            (t1_hbm, t1_raw), (t2_hbm, t2_raw), (t3_hbm, t3_raw), (t4_hbm, t4_raw), (tw_hbm, tw_ref),
        ])
    ]
    for load in loads:
        load.start()
    own = pltpu.make_async_copy(w_ref, wown, own_sem)
    own.start()
    for load in loads[:3]:
        load.wait()

    ut = (k_ref[...].astype(f32) * v_ref[...].astype(f32)).T
    ht = taps_ref[...].T
    both = jnp.concatenate([ut.reshape(BLOCKS, CH, SPAN), ht.reshape(BLOCKS, CH, SPAN)], 1).astype(bf16)
    both = both.reshape(4, 16, 2, 2 * CH, SPAN)
    for i in range(8):
        s1[i] = both[i // 2, :, i % 2]

    for load in loads[4:]:
        load.wait()
    hi, lo = split(t1_raw[...])
    t1_ref[:, 0:128] = hi
    t1_ref[:, 128:256] = lo
    for raw, ref in ((t2_raw, t2_ref), (t3_raw, t3_ref)):
        hi, lo = split(raw[...])
        ref[0:256, :] = hi
        ref[256:512, :] = hi
        ref[512:768, :] = lo
    hi, lo = split(t4_raw[...])
    t4_ref[:, 0:256] = hi
    t4_ref[:, 256:512] = hi
    t4_ref[:, 512:768] = lo

    pl.semaphore_wait(barrier, 30)

    def p1(i, src, dst, ss, rs):
        to = (zk + i) % 8
        return remote(src.at[to], dst.at[zk], ss.at[to], rs.at[zk], dev(to // 2, xy, to % 2, g))

    def p1_from(i, src, dst, ss, rs):
        fr = (zk + 8 - i) % 8
        return remote(src.at[fr], dst.at[fr], ss.at[fr], rs.at[fr], dev(fr // 2, xy, fr % 2, g))

    def p2(i, src, dst, ss, rs):
        to = (xy + i) % 16
        return remote(src.at[:, to], dst.at[xy], ss.at[to], rs.at[xy], dev(z, to, k, g))

    def p2_from(i, src, dst, ss, rs):
        fr = (xy + 16 - i) % 16
        return remote(src.at[:, fr], dst.at[fr], ss.at[fr], rs.at[fr], dev(z, fr, k, g))

    def p3(i):
        to = (xy + i) % 16
        return remote(s3.at[to], r3.at[xy], p3_s.at[to], p3_r.at[xy], dev(z, to, k, g))

    def p3_from(i):
        fr = (xy + 16 - i) % 16
        return remote(s3.at[fr], r3.at[fr], p3_s.at[fr], p3_r.at[fr], dev(z, fr, k, g))

    def p4(i, group):
        to = (zk + i) % 8
        return remote(
            r3.at[:, to], r4.at[g, z, :, k], p4_s.at[group, to], p4_r.at[g, zk], dev(to // 2, xy, to % 2, group)
        )

    def p4_from(i, group):
        fr = (zk + 8 - i) % 8
        return remote(
            r3.at[:, fr], r4.at[group, fr // 2, :, fr % 2], p4_s.at[group, fr], p4_r.at[group, fr],
            dev(fr // 2, xy, fr % 2, group),
        )

    def uv(h):
        return (x, y) if h == 0 else (y, x)

    def place(h, u, v):
        return u % 4 * 4 + v % 4 if h == 0 else v % 4 * 4 + u % 4

    def block(h, sub, at):
        return wo.at[h, sub, k * 16 + at]

    outer = (z + 1) % 4 < 2
    step = z // 2 * 2 - 1

    def fresh(h, sub, far):
        zn = (g * 4 + z + (1 + far) * step + 8) % 8
        src = w_ref.at[
            pl.ds(pl.multiple_of((k * 16 + xy) * 16, 16), 16), pl.ds((h * 2 + sub) * QUARTER, QUARTER)
        ]
        return remote(src, block(h, sub, xy), fresh_s.at[far, h, sub], seed_r.at[h, sub], dev(zn % 4, xy, k, zn // 4))

    def st1(h, side, sub):
        u, v = uv(h)
        to = place(h, u + 1 + side, v)
        return remote(
            block(h, sub, xy), block(h, sub, xy), st1_s.at[h, side, sub], st1_r.at[h, side, sub], dev(z, to, k, g)
        )

    def st2(h, e, side, sub, off=0):
        u, v = uv(h)
        at = place(h, u + e + 4, v + off + 4)
        slot = 0 if off == 0 else 1
        to = place(h, u, v + (1 if side == 0 else 3))
        return remote(
            block(h, sub, at), block(h, sub, at), st2_s.at[h, e % 4, slot, side, sub], st2_r.at[h, e % 4, slot, side, sub],
            dev(z, to, k, g),
        )

    def d2d(h, at, core):
        return remote(
            wo.at[h, :, core * 16 + at], wo.at[h, :, core * 16 + at], d2d_s.at[h, at], d2d_r.at[h, at], dev(z, xy, 1 - k, g)
        )

    def spread(h, e, sub):
        for side in (0, 1):
            st2(h, e, side, sub).start()

    def seed_step(h, sub):
        fresh(h, sub, 0).wait_recv()
        for side in (0, 1, 2):
            st1(h, side, sub).start()
        spread(h, 0, sub)
        if sub == 1:
            d2d(h, xy, k).start()

    def ring1(h, sub):
        u, v = uv(h)
        for side, e in ((0, -1), (2, 1), (1, 2)):
            st1(h, side, sub).wait_recv()
            spread(h, e, sub)
            if sub == 1:
                d2d(h, place(h, u + e + 4, v), k).start()

    def ring2(h, e):
        u, v = uv(h)
        for sub in (0, 1):
            st2(h, e, 0, sub).wait_recv()
            if sub == 0:
                st2(h, e, 0, 0, -1).start()
            st2(h, e, 1, sub).wait_recv()
            if sub == 1:
                st2(h, e, 1, 1, 1).start()
        d2d(h, place(h, u + e + 4, v + 3), k).start()
        d2d(h, place(h, u + e + 4, v + 1), k).start()

    def ring2_far(h, e):
        u, v = uv(h)
        st2(h, e, 0, 0, -1).wait_recv()
        st2(h, e, 1, 1, 1).wait_recv()
        d2d(h, place(h, u + e + 4, v + 2), k).start()

    def in1():
        @pl.loop(1, 8)
        def _(i):
            p1(i, s1, r1, p1_s, p1_r).start()

        r1[zk] = s1[zk]

    def in1q():
        loads[3].wait()
        qt = q_ref[...].astype(f32).T.reshape(BLOCKS, CH, SPAN).astype(bf16).reshape(4, 16, 2, CH, SPAN)
        for i in range(8):
            s1q[i] = qt[i // 2, :, i % 2]

        @pl.loop(1, 8)
        def _(i):
            p1(i, s1q, r1q, p1q_s, p1q_r).start()

        r1q[zk] = s1q[zk]

    def in2():
        @pl.loop(1, 8)
        def _(i):
            p1_from(i, s1, r1, p1_s, p1_r).wait_recv()

        @pl.loop(1, 16)
        def _(i):
            p2(i, r1, r2, p2_s, p2_r).start()

        r2[xy] = r1[:, xy]

    def in2q():
        @pl.loop(1, 8)
        def _(i):
            p1_from(i, s1q, r1q, p1q_s, p1q_r).wait_recv()

        @pl.loop(1, 16)
        def _(i):
            p2(i, r1q, r2q, p2q_s, p2q_r).start()

        r2q[xy] = r1q[:, xy]

    def forward():
        @pl.loop(1, 16)
        def _(i):
            p2_from(i, r1, r2, p2_s, p2_r).wait_recv()

        rows8[...] = r2[...].reshape(BLOCKS, 2 * CH, SPAN).astype(f32).reshape(BLOCKS * 2 * CH, SPAN)
        for r in range(2 * CH):
            part = rows8[pl.ds(r, BLOCKS, stride=2 * CH), :].astype(bf16)
            xcat[0:BLOCKS, r * SPAN : (r + 1) * SPAN] = part
            xcat[BLOCKS : 2 * BLOCKS, r * SPAN : (r + 1) * SPAN] = part
        for r in range(2 * CH):
            got = jnp.dot(t1_ref[...], xcat[:, r * SPAN : (r + 1) * SPAN], preferred_element_type=f32)
            re, im = got[:BLOCKS], got[BLOCKS:]
            hi, lo = split(jnp.concatenate([re * tw_ref[0] - im * tw_ref[1], re * tw_ref[1] + im * tw_ref[0]], 1))
            lhs2[r * BLOCKS : (r + 1) * BLOCKS, 0:256] = hi
            lhs2[r * BLOCKS : (r + 1) * BLOCKS, 256:512] = lo
            lhs2[r * BLOCKS : (r + 1) * BLOCKS, 512:768] = hi

    def middle():
        for c in range(CH):
            rows = pl.ds(c * BLOCKS, BLOCKS)
            left = jnp.dot(lhs2[rows, :], t2_ref[...], preferred_element_type=f32)
            right = jnp.dot(lhs2[pl.ds((c + CH) * BLOCKS, BLOCKS), :], t2_ref[...], preferred_element_type=f32)
            lr, li, rr, ri = left[:, :SPAN], left[:, SPAN:], right[:, :SPAN], right[:, SPAN:]
            hi, lo = split(jnp.concatenate([lr * rr - li * ri, lr * ri + li * rr], 1))
            lhs3[rows, 0:256] = hi
            lhs3[rows, 256:512] = lo
            lhs3[rows, 512:768] = hi
        for c in range(CH):
            rows = pl.ds(c * BLOCKS, BLOCKS)
            got = jnp.dot(lhs3[rows, :], t3_ref[...], preferred_element_type=f32)
            re, im = got[:, :SPAN], got[:, SPAN:]
            cols = pl.ds(c * SPAN, SPAN)
            hi, lo = split(jnp.concatenate([re * tw_ref[0] + im * tw_ref[1], im * tw_ref[0] - re * tw_ref[1]], 0))
            rhs4[0:256, cols] = hi
            rhs4[256:512, cols] = lo
            rhs4[512:768, cols] = hi

    def out1():
        @pl.loop(1, 16)
        def _(i):
            p2_from(i, r1q, r2q, p2q_s, p2q_r).wait_recv()

        rows4[...] = r2q[...].reshape(BLOCKS, CH, SPAN).astype(f32).reshape(BLOCKS * CH, SPAN)
        for c in range(CH):
            conv = jnp.dot(t4_ref[...], rhs4[:, c * SPAN : (c + 1) * SPAN], preferred_element_type=f32)
            at = pl.ds(c, BLOCKS, stride=CH)
            signal = rows8[pl.ds(c, BLOCKS, stride=2 * CH), :]
            rows4[at, :] = rows4[at, :] * (conv + skip_ref[0, me * CH + c] * signal)
        s3[...] = rows4[...].astype(bf16).reshape(16, 8, CH, SPAN)

        @pl.loop(1, 16)
        def _(i):
            p3(i).start()

        r3[xy] = s3[xy]

    def out2():
        @pl.loop(1, 16)
        def _(i):
            p3_from(i).wait_recv()

        @pl.loop(1, 8)
        def _(i):
            p4(i, g).start()

        @pl.loop(0, 8)
        def _(i):
            p4(i, 1 - g).start()

        r4[g, z, :, k] = r3[:, zk]

    def project_here():
        @pl.loop(1, 8)
        def _(i):
            p4_from(i, g).wait_recv()

        own.wait()
        here = r4[g].reshape(512, SPAN).T

        @pl.loop(0, 16)
        def _(t):
            cols = pl.ds(pl.multiple_of(t * TILE, TILE), TILE)
            acc[:, cols] = jnp.dot(here, wown[:, cols], preferred_element_type=f32)

    def leave(part, t):
        cols = pl.ds(part * QUARTER + t * TILE, TILE)
        return pltpu.make_async_copy(result.at[:, cols], out_ref.at[:, cols], out_sem.at[part, t])

    def project_there():
        @pl.loop(0, 8)
        def _(i):
            p4_from(i, 1 - g).wait_recv()

        there = r4[1 - g].reshape(512, SPAN).T
        for part in range(4):
            if part % 2 == 0:

                @pl.loop(0, 16)
                def _(i):
                    d2d(part // 2, i, 1 - k).wait_recv()

            for t in range(QUARTER // TILE):
                base = part * QUARTER + t * TILE
                weight = wo[part // 2, part % 2, :, :, t * TILE : (t + 1) * TILE].reshape(512, TILE)
                total = acc[:, base : base + TILE] + jnp.dot(there, weight, preferred_element_type=f32)
                result[:, base : base + TILE] = total.astype(bf16)
                leave(part, t).start()


    @pl.when(outer)
    def _():
        for sub in (0, 1):
            for h in (0, 1):
                for far in (0, 1):
                    fresh(h, sub, far).start()

    in1()
    in1q()
    seed_step(0, 0)
    seed_step(1, 0)
    in2()
    seed_step(0, 1)
    in2q()
    ring1(0, 0)
    seed_step(1, 1)
    ring1(1, 0)
    forward()
    ring1(0, 1)
    middle()
    out1()
    ring1(1, 1)
    ring2(0, 0)
    ring2(1, 0)
    out2()
    for e in (-1, 1, 2):
        for h in (0, 1):
            ring2(h, e)
    project_here()
    for e in (0, -1, 1, 2):
        for h in (0, 1):
            ring2_far(h, e)
    project_there()

    @pl.loop(1, 8)
    def _(i):
        p1(i, s1, r1, p1_s, p1_r).wait_send()
        p1(i, s1q, r1q, p1q_s, p1q_r).wait_send()
        p4(i, g).wait_send()

    @pl.loop(1, 16)
    def _(i):
        p2(i, r1, r2, p2_s, p2_r).wait_send()
        p2(i, r1q, r2q, p2q_s, p2q_r).wait_send()
        p3(i).wait_send()

    @pl.loop(0, 8)
    def _(i):
        p4(i, 1 - g).wait_send()

    @pl.loop(0, 16)
    def _(i):
        d2d(0, i, k).wait_send()
        d2d(1, i, k).wait_send()

    @pl.when(outer)
    def _():
        for h in (0, 1):
            for sub in (0, 1):
                for far in (0, 1):
                    fresh(h, sub, far).wait_send()

    for h in (0, 1):
        for sub in (0, 1):
            for side in (0, 1, 2):
                st1(h, side, sub).wait_send()
            for side in (0, 1):
                for e in (0, -1, 1, 2):
                    st2(h, e, side, sub).wait_send()
        for e in (0, -1, 1, 2):
            st2(h, e, 0, 0, -1).wait_send()
            st2(h, e, 1, 1, 1).wait_send()
    for part in range(4):
        for t in range(QUARTER // TILE):
            leave(part, t).wait()


def body(query_branch, key_branch, value_branch, filter_taps, skip_gain, out_weight):
    width = out_weight.shape[1]
    hbm = pl.BlockSpec(memory_space=pltpu.HBM)
    dma = pltpu.SemaphoreType.DMA
    v = pltpu.VMEM
    consts = tables()
    return pl.pallas_call(
        kernel,
        out_shape=jax.ShapeDtypeStruct((SPAN, width), bf16),
        in_specs=[hbm] * 4 + [pl.BlockSpec(memory_space=pltpu.SMEM)] + [hbm] * 6,
        out_specs=hbm,
        scratch_shapes=[
            v((SPAN, 512), bf16), v((SPAN, 512), bf16), v((SPAN, 512), bf16), v((SPAN, 512), f32),
            *[v(t.shape, t.dtype) for t in consts], dma((9,)),
            v((256, 256), bf16), v((768, 256), bf16), v((768, 256), bf16), v((128, 768), bf16),
            v((8, 16, 2 * CH, SPAN), bf16), v((8, 16, 2 * CH, SPAN), bf16), v((16, 8, 2 * CH, SPAN), bf16),
            v((8, 16, CH, SPAN), bf16), v((8, 16, CH, SPAN), bf16), v((16, 8, CH, SPAN), bf16),
            v((16, 8, CH, SPAN), bf16), v((16, 8, CH, SPAN), bf16), v((2, 4, 16, 2, CH, SPAN), bf16),
            v((512, width), bf16), v((2, 2, 32, 16, QUARTER), bf16), v((SPAN, width), f32),
            v((BLOCKS * 2 * CH, SPAN), f32), v((BLOCKS * CH, SPAN), f32),
            v((256, 2 * CH * SPAN), bf16), v((2 * CH * BLOCKS, 768), bf16), v((CH * BLOCKS, 768), bf16), v((768, CH * SPAN), bf16),
            dma, dma((8,)), dma((8,)), dma((8,)), dma((8,)), dma((16,)), dma((16,)), dma((16,)), dma((16,)),
            dma((16,)), dma((16,)), dma((2, 8)), dma((2, 8)),
            dma((2, 2, 2)), dma((2, 2)), dma((2, 3, 2)), dma((2, 3, 2)), dma((2, 4, 2, 2, 2)), dma((2, 4, 2, 2, 2)),
            dma((2, 16)), dma((2, 16)), v((SPAN, width), bf16), dma((4, QUARTER // TILE)),
        ],
        compiler_params=pltpu.CompilerParams(collective_id=0, has_side_effects=True, vmem_limit_bytes=56 * 2**20),
    )(query_branch, key_branch, value_branch, filter_taps, skip_gain.reshape(1, -1), *consts, out_weight)
def solution(mesh):
    return jax.shard_map(
        body,
        mesh=mesh,
        in_specs=(P("seq", "ch"), P("seq", "ch"), P("seq", "ch"), P("seq", "ch"), P("ch"), P("ch", None)),
        out_specs=P("seq", None),
        check_vma=False,
    )
```

```python
import functools
import math

import jax
import jax.numpy as jnp
import numpy as np
from jax import lax
from jax.experimental import pallas as pl
from jax.experimental.pallas import tpu as pltpu
from jax.sharding import PartitionSpec as P

bf16 = jnp.bfloat16
f32 = jnp.float32
MESH = pl.DeviceIdType.MESH
SPAN = 128
BLOCKS = 128
CH = 4
TILE = 512
QUARTER = 2048


def split(t):
    hi = t.astype(bf16)
    return hi, (t - hi.astype(f32)).astype(bf16)


def tables():
    n = 2 * BLOCKS
    at = np.arange(BLOCKS)
    a = (at % 8) // 2 * 32 + at // 8 * 2 + at % 2
    alpha = np.arange(BLOCKS)[:, None] + 0.5
    fine = np.arange(SPAN)
    ahead = 2.0 * np.pi * alpha * a[None, :] / n
    turn = 2.0 * np.pi * alpha * fine[None, :] / (n * SPAN)
    inner = 2.0 * np.pi * (fine[:, None] * fine[None, :] % SPAN) / SPAN
    first = np.concatenate([np.cos(ahead), -np.sin(ahead)], 0)
    second = np.block([[np.cos(inner), -np.sin(inner)], [np.sin(inner), np.cos(inner)]])
    back = np.block([[np.cos(inner), np.sin(inner)], [-np.sin(inner), np.cos(inner)]])
    last = first.T / (BLOCKS * SPAN)

    as32 = lambda t: jnp.asarray(t.astype(np.float32))
    return as32(first), as32(second), as32(back), as32(last), as32(np.stack([np.cos(turn), -np.sin(turn)]))


def kernel(
    q_hbm, k_hbm, v_hbm, taps_hbm, skip_ref, t1_hbm, t2_hbm, t3_hbm, t4_hbm, tw_hbm, w_ref, out_ref,
    q_ref, k_ref, v_ref, taps_ref, t1_raw, t2_raw, t3_raw, t4_raw, tw_ref, load_sem, t1_ref, t2_ref, t3_ref, t4_ref,
    s1, r1, r2, s1q, r1q, r2q, s3, r3, r4, wown, wo, acc, rows8, rows4, xcat, lhs2, lhs3, rhs4,
    own_sem, p1_s, p1_r, p1q_s, p1q_r, p2_s, p2_r, p2q_s, p2q_r, p3_s, p3_r, p4_s, p4_r,
    ring_s, fresh_s, seed_r, st1_r, st2_r, far_r, d2d_s, d2d_r, result, out_sem,
):
    me = lax.axis_index("seq")
    g = lax.axis_index("ch")
    z, xy, k = me // 32, me // 2 % 16, me % 2
    x, y = xy // 4, xy % 4
    zk = z * 2 + k

    def dev(z_, xy_, k_, g_):
        return (z_ * 32 + xy_ * 2 + k_, g_)

    def remote(src, dst, ss, rs, to):
        return pltpu.make_async_remote_copy(
            src_ref=src, dst_ref=dst, send_sem=ss, recv_sem=rs, device_id=to, device_id_type=MESH
        )

    barrier = pltpu.get_barrier_semaphore()

    @pl.loop(1, 16)
    def _(i):
        pl.semaphore_signal(barrier, inc=1, device_id=dev(z, (xy + i) % 16, k, g), device_id_type=MESH)

    @pl.loop(1, 8)
    def _(i):
        to = (zk + i) % 8
        pl.semaphore_signal(barrier, inc=1, device_id=dev(to // 2, xy, to % 2, g), device_id_type=MESH)

    @pl.loop(0, 8)
    def _(i):
        pl.semaphore_signal(barrier, inc=1, device_id=dev(i // 2, xy, i % 2, 1 - g), device_id_type=MESH)

    loads = [
        pltpu.make_async_copy(src, dst, load_sem.at[i])
        for i, (src, dst) in enumerate([
            (k_hbm, k_ref), (v_hbm, v_ref), (taps_hbm, taps_ref), (q_hbm, q_ref),
            (t1_hbm, t1_raw), (t2_hbm, t2_raw), (t3_hbm, t3_raw), (t4_hbm, t4_raw), (tw_hbm, tw_ref),
        ])
    ]
    for load in loads:
        load.start()
    own = pltpu.make_async_copy(w_ref, wown, own_sem)
    own.start()
    for load in loads[:3]:
        load.wait()

    ut = (k_ref[...].astype(f32) * v_ref[...].astype(f32)).T
    ht = taps_ref[...].T
    both = jnp.concatenate([ut.reshape(BLOCKS, CH, SPAN), ht.reshape(BLOCKS, CH, SPAN)], 1).astype(bf16)
    both = both.reshape(4, 16, 2, 2 * CH, SPAN)
    for i in range(8):
        s1[i] = both[i // 2, :, i % 2]

    for load in loads[4:]:
        load.wait()
    hi, lo = split(t1_raw[...])
    t1_ref[:, 0:128] = hi
    t1_ref[:, 128:256] = lo
    for raw, ref in ((t2_raw, t2_ref), (t3_raw, t3_ref)):
        hi, lo = split(raw[...])
        ref[0:256, :] = hi
        ref[256:512, :] = hi
        ref[512:768, :] = lo
    hi, lo = split(t4_raw[...])
    t4_ref[:, 0:256] = hi
    t4_ref[:, 256:512] = hi
    t4_ref[:, 512:768] = lo

    pl.semaphore_wait(barrier, 30)

    def p1(i, src, dst, ss, rs):
        to = (zk + i) % 8
        return remote(src.at[to], dst.at[zk], ss, rs, dev(to // 2, xy, to % 2, g))

    def p2(i, src, dst, ss, rs):
        to = (xy + i) % 16
        return remote(src.at[:, to], dst.at[xy], ss, rs, dev(z, to, k, g))

    def p3(i):
        to = (xy + i) % 16
        return remote(s3.at[to], r3.at[xy], p3_s, p3_r, dev(z, to, k, g))

    def p4(i, group):
        to = (zk + i) % 8
        return remote(r3.at[:, to], r4.at[g, z, :, k], p4_s.at[group], p4_r.at[g], dev(to // 2, xy, to % 2, group))

    def all_of(ref, ss, rs):
        return remote(ref, ref, ss, rs, dev(z, xy, 1 - k, g))

    def uv(h):
        return (x, y) if h == 0 else (y, x)

    def place(h, u, v):
        return u % 4 * 4 + v % 4 if h == 0 else v % 4 * 4 + u % 4

    def block(h, sub, at):
        return wo.at[h, sub, k * 16 + at]

    outer = (z + 1) % 4 < 2
    step = z // 2 * 2 - 1

    zn, zf = (g * 4 + z + step + 8) % 8, (g * 4 + z + 2 * step + 8) % 8
    beyond = (dev(zn % 4, xy, k, zn // 4), dev(zf % 4, xy, k, zf // 4))

    def fresh(h, sub, far):
        src = w_ref.at[
            pl.ds(pl.multiple_of((k * 16 + xy) * 16, 16), 16), pl.ds((h * 2 + sub) * QUARTER, QUARTER)
        ]
        return remote(src, block(h, sub, xy), fresh_s, seed_r.at[h, sub], beyond[far])

    def st1(h, side, sub):
        u, v = uv(h)
        to = place(h, u + 1 + side, v)
        return remote(block(h, sub, xy), block(h, sub, xy), ring_s, st1_r.at[h], dev(z, to, k, g))

    def st2(h, e, side):
        u, v = uv(h)
        there = wo.at[h, :, k * 16 + place(h, u + e + 4, v)]
        to = place(h, u, v + (1 if side == 0 else 3))
        return remote(there, there, ring_s, st2_r.at[h, e % 4], dev(z, to, k, g))

    def st2_on(h, e, side):
        u, v = uv(h)
        there = block(h, side, place(h, u + e + 4, v + (3 if side == 0 else 1)))
        to = place(h, u, v + (1 if side == 0 else 3))
        return remote(there, there, ring_s, far_r.at[h, e % 4], dev(z, to, k, g))

    def d2d(h, at):
        there = wo.at[h, :, k * 16 + at]
        return remote(there, there, d2d_s, d2d_r.at[h], dev(z, xy, 1 - k, g))

    def spread(h, e):
        for side in (0, 1):
            st2(h, e, side).start()

    def seed_step(h, sub):
        all_of(wo.at[0, 0, 0], fresh_s, seed_r.at[h, sub]).wait_recv()
        for side in (0, 1, 2):
            st1(h, side, sub).start()
        if sub == 1:
            d2d(h, xy).start()

    def ring1(h):
        u, v = uv(h)
        all_of(wo.at[0, 0, 0:6], ring_s, st1_r.at[h]).wait_recv()
        for e in (-1, 1, 2):
            spread(h, e)
        for e in (-1, 1, 2):
            d2d(h, place(h, u + e + 4, v)).start()

    def ring2(h, e):
        u, v = uv(h)
        all_of(wo.at[0, 0, 0:4], ring_s, st2_r.at[h, e % 4]).wait_recv()
        for side in (0, 1):
            st2_on(h, e, side).start()
        for off in (1, 3):
            d2d(h, place(h, u + e + 4, v + off)).start()

    def ring2_far(h, e):
        u, v = uv(h)
        all_of(wo.at[0, 0, 0:2], ring_s, far_r.at[h, e % 4]).wait_recv()
        d2d(h, place(h, u + e + 4, v + 2)).start()

    def in1():
        @pl.loop(1, 8)
        def _(i):
            p1(i, s1, r1, p1_s, p1_r).start()

        r1[zk] = s1[zk]

    def in1q():
        loads[3].wait()
        qt = q_ref[...].astype(f32).T.reshape(BLOCKS, CH, SPAN).astype(bf16).reshape(4, 16, 2, CH, SPAN)
        for i in range(8):
            s1q[i] = qt[i // 2, :, i % 2]

    def in1q_send():
        @pl.loop(1, 8)
        def _(i):
            p1(i, s1q, r1q, p1q_s, p1q_r).start()

        r1q[zk] = s1q[zk]

    def in2():
        all_of(r1.at[0:7], p1_s, p1_r).wait_recv()

        @pl.loop(1, 16)
        def _(i):
            p2(i, r1, r2, p2_s, p2_r).start()

        r2[xy] = r1[:, xy]

    def in2q():
        all_of(r1q.at[0:7], p1q_s, p1q_r).wait_recv()

        @pl.loop(1, 16)
        def _(i):
            p2(i, r1q, r2q, p2q_s, p2q_r).start()

        r2q[xy] = r1q[:, xy]

    def forward():
        all_of(r2.at[0:15], p2_s, p2_r).wait_recv()

        rows8[...] = r2[...].reshape(BLOCKS, 2 * CH, SPAN).astype(f32).reshape(BLOCKS * 2 * CH, SPAN)
        for r in range(2 * CH):
            part = rows8[pl.ds(r, BLOCKS, stride=2 * CH), :].astype(bf16)
            xcat[0:BLOCKS, r * SPAN : (r + 1) * SPAN] = part
            xcat[BLOCKS : 2 * BLOCKS, r * SPAN : (r + 1) * SPAN] = part
        for r in range(2 * CH):
            got = jnp.dot(t1_ref[...], xcat[:, r * SPAN : (r + 1) * SPAN], preferred_element_type=f32)
            re, im = got[:BLOCKS], got[BLOCKS:]
            hi, lo = split(jnp.concatenate([re * tw_ref[0] - im * tw_ref[1], re * tw_ref[1] + im * tw_ref[0]], 1))
            lhs2[r * BLOCKS : (r + 1) * BLOCKS, 0:256] = hi
            lhs2[r * BLOCKS : (r + 1) * BLOCKS, 256:512] = lo
            lhs2[r * BLOCKS : (r + 1) * BLOCKS, 512:768] = hi

    def middle():
        for c in range(CH):
            rows = pl.ds(c * BLOCKS, BLOCKS)
            left = jnp.dot(lhs2[rows, :], t2_ref[...], preferred_element_type=f32)
            right = jnp.dot(lhs2[pl.ds((c + CH) * BLOCKS, BLOCKS), :], t2_ref[...], preferred_element_type=f32)
            lr, li, rr, ri = left[:, :SPAN], left[:, SPAN:], right[:, :SPAN], right[:, SPAN:]
            hi, lo = split(jnp.concatenate([lr * rr - li * ri, lr * ri + li * rr], 1))
            lhs3[rows, 0:256] = hi
            lhs3[rows, 256:512] = lo
            lhs3[rows, 512:768] = hi
        for c in range(CH):
            rows = pl.ds(c * BLOCKS, BLOCKS)
            got = jnp.dot(lhs3[rows, :], t3_ref[...], preferred_element_type=f32)
            re, im = got[:, :SPAN], got[:, SPAN:]
            cols = pl.ds(c * SPAN, SPAN)
            hi, lo = split(jnp.concatenate([re * tw_ref[0] + im * tw_ref[1], im * tw_ref[0] - re * tw_ref[1]], 0))
            rhs4[0:256, cols] = hi
            rhs4[256:512, cols] = lo
            rhs4[512:768, cols] = hi

    def out1():
        all_of(r2q.at[0:15], p2q_s, p2q_r).wait_recv()

        rows4[...] = r2q[...].reshape(BLOCKS, CH, SPAN).astype(f32).reshape(BLOCKS * CH, SPAN)
        for c in range(CH):
            conv = jnp.dot(t4_ref[...], rhs4[:, c * SPAN : (c + 1) * SPAN], preferred_element_type=f32)
            at = pl.ds(c, BLOCKS, stride=CH)
            signal = rows8[pl.ds(c, BLOCKS, stride=2 * CH), :]
            rows4[at, :] = rows4[at, :] * (conv + skip_ref[0, me * CH + c] * signal)
        s3[...] = rows4[...].astype(bf16).reshape(16, 8, CH, SPAN)

        @pl.loop(1, 16)
        def _(i):
            p3(i).start()

        r3[xy] = s3[xy]

    def out2():
        all_of(r3.at[0:15], p3_s, p3_r).wait_recv()

        @pl.loop(1, 8)
        def _(i):
            p4(i, g).start()

        @pl.loop(0, 8)
        def _(i):
            p4(i, 1 - g).start()

        r4[g, z, :, k] = r3[:, zk]

    def project_here():
        all_of(r3.at[0:14], p4_s.at[g], p4_r.at[g]).wait_recv()

        own.wait()
        here = r4[g].reshape(512, SPAN).T

        @pl.loop(0, 16)
        def _(t):
            cols = pl.ds(pl.multiple_of(t * TILE, TILE), TILE)
            acc[:, cols] = jnp.dot(here, wown[:, cols], preferred_element_type=f32)

    def leave(i, base, size):
        cols = pl.ds(base, size)
        return pltpu.make_async_copy(result.at[:, cols], out_ref.at[:, cols], out_sem.at[i])

    leaving = [(t * TILE, TILE) for t in range(16)]

    def project_there():
        all_of(r3, p4_s.at[1 - g], p4_r.at[1 - g]).wait_recv()

        there = r4[1 - g].reshape(512, SPAN).T

        def finish(i, weight):
            base, size = leaving[i]
            total = acc[:, base : base + size] + jnp.dot(there, weight.reshape(512, size), preferred_element_type=f32)
            result[:, base : base + size] = total.astype(bf16)
            leave(i, base, size).start()

        for part in range(4):
            if part % 2 == 0:

                all_of(wo.at[0, :, 0:16], d2d_s, d2d_r.at[part // 2]).wait_recv()

            for t in range(4):
                finish(part * 4 + t, wo[part // 2, part % 2, :, :, t * TILE : (t + 1) * TILE])

    def sent():
        all_of(s1.at[0:7], p1_s, p1_r).wait_send()
        all_of(s1q.at[0:7], p1q_s, p1q_r).wait_send()
        all_of(r2.at[0:15], p2_s, p2_r).wait_send()
        all_of(r2q.at[0:15], p2q_s, p2q_r).wait_send()
        all_of(s3.at[0:15], p3_s, p3_r).wait_send()

        @pl.when(outer)
        def _():
            all_of(wo.at[0, 0, 0:8], fresh_s, seed_r.at[0, 0]).wait_send()


    @pl.when(outer)
    def _():
        for sub in (0, 1):
            for h in (0, 1):
                for far in (0, 1):
                    fresh(h, sub, far).start()

    in1()
    in1q()
    in1q_send()
    seed_step(0, 0)
    seed_step(1, 0)
    in2()
    seed_step(0, 1)
    in2q()
    seed_step(1, 1)
    forward()
    spread(0, 0)
    spread(1, 0)
    middle()
    out1()
    ring1(0)
    ring1(1)
    out2()
    for e in (0, -1, 1, 2):
        for h in (0, 1):
            ring2(h, e)
    project_here()
    sent()
    for e in (0, -1, 1, 2):
        for h in (0, 1):
            ring2_far(h, e)
    project_there()

    all_of(r3.at[0:14], p4_s.at[g], p4_r.at[g]).wait_send()
    all_of(r3, p4_s.at[1 - g], p4_r.at[1 - g]).wait_send()
    all_of(wo.at[:, :, 0:16], d2d_s, d2d_r.at[0]).wait_send()
    all_of(wo.at[:, :, 0:15], ring_s, st1_r.at[0]).wait_send()
    for i, (base, size) in enumerate(leaving):
        leave(i, base, size).wait()


def body(query_branch, key_branch, value_branch, filter_taps, skip_gain, out_weight):
    width = out_weight.shape[1]
    hbm = pl.BlockSpec(memory_space=pltpu.HBM)
    dma = pltpu.SemaphoreType.DMA
    v = pltpu.VMEM
    consts = tables()
    return pl.pallas_call(
        kernel,
        out_shape=jax.ShapeDtypeStruct((SPAN, width), bf16),
        in_specs=[hbm] * 4 + [pl.BlockSpec(memory_space=pltpu.SMEM)] + [hbm] * 6,
        out_specs=hbm,
        scratch_shapes=[
            v((SPAN, 512), bf16), v((SPAN, 512), bf16), v((SPAN, 512), bf16), v((SPAN, 512), f32),
            *[v(t.shape, t.dtype) for t in consts], dma((9,)),
            v((256, 256), bf16), v((768, 256), bf16), v((768, 256), bf16), v((128, 768), bf16),
            v((8, 16, 2 * CH, SPAN), bf16), v((8, 16, 2 * CH, SPAN), bf16), v((16, 8, 2 * CH, SPAN), bf16),
            v((8, 16, CH, SPAN), bf16), v((8, 16, CH, SPAN), bf16), v((16, 8, CH, SPAN), bf16),
            v((16, 8, CH, SPAN), bf16), v((16, 8, CH, SPAN), bf16), v((2, 4, 16, 2, CH, SPAN), bf16),
            v((512, width), bf16), v((2, 2, 32, 16, QUARTER), bf16), v((SPAN, width), f32),
            v((BLOCKS * 2 * CH, SPAN), f32), v((BLOCKS * CH, SPAN), f32),
            v((256, 2 * CH * SPAN), bf16), v((2 * CH * BLOCKS, 768), bf16), v((CH * BLOCKS, 768), bf16), v((768, CH * SPAN), bf16),
            dma, dma, dma, dma, dma, dma, dma, dma, dma, dma, dma, dma((2,)), dma((2,)),
            dma, dma, dma((2, 2)), dma((2,)), dma((2, 4)), dma((2, 4)), dma, dma((2,)), v((SPAN, width), bf16), dma((16,)),
        ],
        compiler_params=pltpu.CompilerParams(collective_id=0, has_side_effects=True, vmem_limit_bytes=56 * 2**20),
    )(query_branch, key_branch, value_branch, filter_taps, skip_gain.reshape(1, -1), *consts, out_weight)
def solution(mesh):
    return jax.shard_map(
        body,
        mesh=mesh,
        in_specs=(P("seq", "ch"), P("seq", "ch"), P("seq", "ch"), P("seq", "ch"), P("ch"), P("ch", None)),
        out_specs=P("seq", None),
        check_vma=False,
    )
```

```python
import functools
import math

import jax
import jax.numpy as jnp
import numpy as np
from jax import lax
from jax.experimental import pallas as pl
from jax.experimental.pallas import tpu as pltpu
from jax.sharding import PartitionSpec as P

bf16 = jnp.bfloat16
f32 = jnp.float32
MESH = pl.DeviceIdType.MESH
SPAN = 128
BLOCKS = 128
CH = 4
TILE = 512
QUARTER = 2048


def split(t):
    hi = t.astype(bf16)
    return hi, (t - hi.astype(f32)).astype(bf16)


def tables():
    n = 2 * BLOCKS
    at = np.arange(BLOCKS)
    a = (at % 8) // 2 * 32 + at // 8 * 2 + at % 2
    alpha = np.arange(BLOCKS)[:, None] + 0.5
    fine = np.arange(SPAN)
    ahead = 2.0 * np.pi * alpha * a[None, :] / n
    turn = 2.0 * np.pi * alpha * fine[None, :] / (n * SPAN)
    inner = 2.0 * np.pi * (fine[:, None] * fine[None, :] % SPAN) / SPAN
    first = np.concatenate([np.cos(ahead), -np.sin(ahead)], 0)
    second = np.block([[np.cos(inner), -np.sin(inner)], [np.sin(inner), np.cos(inner)]])
    back = np.block([[np.cos(inner), np.sin(inner)], [-np.sin(inner), np.cos(inner)]])
    last = first.T / (BLOCKS * SPAN)

    as32 = lambda t: jnp.asarray(t.astype(np.float32))
    return as32(first), as32(second), as32(back), as32(last), as32(np.stack([np.cos(turn), -np.sin(turn)]))


def kernel(
    q_hbm, k_hbm, v_hbm, taps_hbm, skip_ref, t1_hbm, t2_hbm, t3_hbm, t4_hbm, tw_hbm, w_ref, out_ref,
    q_ref, k_ref, v_ref, taps_ref, t1_raw, t2_raw, t3_raw, t4_raw, tw_ref, load_sem, t1_ref, t2_ref, t3_ref, t4_ref,
    s1, r1, r2, s1q, r1q, r2q, s3, r3, r4, wown, wo, acc, rows8, rows4, xcat, lhs2, lhs3, rhs4,
    own_sem, p1_s, p1_r, p1q_s, p1q_r, p2_s, p2_r, p2q_s, p2q_r, p3_s, p3_r, p4_s, p4_r,
    ring_s, fresh_s, seed_r, st1_r, st2_r, far_r, d2d_s, d2d_r, result, out_sem,
):
    me = lax.axis_index("seq")
    g = lax.axis_index("ch")
    z, xy, k = me // 32, me // 2 % 16, me % 2
    x, y = xy // 4, xy % 4
    zk = z * 2 + k

    def dev(z_, xy_, k_, g_):
        return (z_ * 32 + xy_ * 2 + k_, g_)

    def remote(src, dst, ss, rs, to):
        return pltpu.make_async_remote_copy(
            src_ref=src, dst_ref=dst, send_sem=ss, recv_sem=rs, device_id=to, device_id_type=MESH
        )

    barrier = pltpu.get_barrier_semaphore()

    @pl.loop(1, 16)
    def _(i):
        pl.semaphore_signal(barrier, inc=1, device_id=dev(z, (xy + i) % 16, k, g), device_id_type=MESH)

    @pl.loop(1, 8)
    def _(i):
        to = (zk + i) % 8
        pl.semaphore_signal(barrier, inc=1, device_id=dev(to // 2, xy, to % 2, g), device_id_type=MESH)

    @pl.loop(0, 8)
    def _(i):
        pl.semaphore_signal(barrier, inc=1, device_id=dev(i // 2, xy, i % 2, 1 - g), device_id_type=MESH)

    loads = [
        pltpu.make_async_copy(src, dst, load_sem.at[i])
        for i, (src, dst) in enumerate([
            (k_hbm, k_ref), (v_hbm, v_ref), (taps_hbm, taps_ref), (q_hbm, q_ref),
            (t1_hbm, t1_raw), (t2_hbm, t2_raw), (t3_hbm, t3_raw), (t4_hbm, t4_raw), (tw_hbm, tw_ref),
        ])
    ]
    for load in loads:
        load.start()
    own = pltpu.make_async_copy(w_ref, wown, own_sem)
    own.start()
    for load in loads[:3]:
        load.wait()

    ut = (k_ref[...].astype(f32) * v_ref[...].astype(f32)).T
    ht = taps_ref[...].T
    both = jnp.concatenate([ut.reshape(BLOCKS, CH, SPAN), ht.reshape(BLOCKS, CH, SPAN)], 1).astype(bf16)
    both = both.reshape(4, 16, 2, 2 * CH, SPAN)
    for i in range(8):
        s1[i] = both[i // 2, :, i % 2]

    for load in loads[4:]:
        load.wait()
    hi, lo = split(t1_raw[...])
    t1_ref[:, 0:128] = hi
    t1_ref[:, 128:256] = lo
    for raw, ref in ((t2_raw, t2_ref), (t3_raw, t3_ref)):
        hi, lo = split(raw[...])
        ref[0:256, :] = hi
        ref[256:512, :] = hi
        ref[512:768, :] = lo
    hi, lo = split(t4_raw[...])
    t4_ref[:, 0:256] = hi
    t4_ref[:, 256:512] = hi
    t4_ref[:, 512:768] = lo

    pl.semaphore_wait(barrier, 30)

    def p1(i, src, dst, ss, rs):
        to = (zk + (z // 2 * 2 - 1) * i + 8) % 8
        return remote(src.at[to], dst.at[zk], ss, rs, dev(to // 2, xy, to % 2, g))

    def p2(i, src, dst, ss, rs):
        to = (xy + i) % 16
        return remote(src.at[:, to], dst.at[xy], ss, rs, dev(z, to, k, g))

    def p3(i):
        to = (xy + i) % 16
        return remote(s3.at[to], r3.at[xy], p3_s, p3_r, dev(z, to, k, g))

    def p4(i, group):
        to = (zk + i) % 8
        return remote(r3.at[:, to], r4.at[g, z, :, k], p4_s.at[group], p4_r.at[g], dev(to // 2, xy, to % 2, group))

    def all_of(ref, ss, rs):
        return remote(ref, ref, ss, rs, dev(z, xy, 1 - k, g))

    def uv(h):
        return (x, y) if h == 0 else (y, x)

    def place(h, u, v):
        return u % 4 * 4 + v % 4 if h == 0 else v % 4 * 4 + u % 4

    def block(h, sub, at):
        return wo.at[h, sub, k * 16 + at]

    outer = (z + 1) % 4 < 2
    step = z // 2 * 2 - 1

    zn, zf = (g * 4 + z + step + 8) % 8, (g * 4 + z + 2 * step + 8) % 8
    beyond = (dev(zn % 4, xy, k, zn // 4), dev(zf % 4, xy, k, zf // 4))

    def fresh(h, sub, far):
        src = w_ref.at[
            pl.ds(pl.multiple_of((k * 16 + xy) * 16, 16), 16), pl.ds((h * 2 + sub) * QUARTER, QUARTER)
        ]
        return remote(src, block(h, sub, xy), fresh_s, seed_r.at[h, sub], beyond[far])

    def st1(h, side, sub):
        u, v = uv(h)
        to = place(h, u + 1 + side, v)
        return remote(block(h, sub, xy), block(h, sub, xy), ring_s, st1_r.at[h], dev(z, to, k, g))

    def st2(h, e, side):
        u, v = uv(h)
        there = wo.at[h, :, k * 16 + place(h, u + e + 4, v)]
        to = place(h, u, v + (1 if side == 0 else 3))
        return remote(there, there, ring_s, st2_r.at[h, e % 4], dev(z, to, k, g))

    def st2_on(h, e, side):
        u, v = uv(h)
        there = block(h, side, place(h, u + e + 4, v + (3 if side == 0 else 1)))
        to = place(h, u, v + (1 if side == 0 else 3))
        return remote(there, there, ring_s, far_r.at[h, e % 4], dev(z, to, k, g))

    def d2d(h, at):
        there = wo.at[h, :, k * 16 + at]
        return remote(there, there, d2d_s, d2d_r.at[h], dev(z, xy, 1 - k, g))

    def spread(h, e):
        for side in (0, 1):
            st2(h, e, side).start()

    def seed_step(h, sub):
        all_of(wo.at[0, 0, 0], fresh_s, seed_r.at[h, sub]).wait_recv()
        for side in (0, 1, 2):
            st1(h, side, sub).start()
        if sub == 1:
            d2d(h, xy).start()

    def ring1(h):
        u, v = uv(h)
        all_of(wo.at[0, 0, 0:6], ring_s, st1_r.at[h]).wait_recv()
        for e in (-1, 1, 2):
            spread(h, e)
        for e in (-1, 1, 2):
            d2d(h, place(h, u + e + 4, v)).start()

    def ring2(h, e):
        u, v = uv(h)
        all_of(wo.at[0, 0, 0:4], ring_s, st2_r.at[h, e % 4]).wait_recv()
        for side in (0, 1):
            st2_on(h, e, side).start()
        for off in (1, 3):
            d2d(h, place(h, u + e + 4, v + off)).start()

    def ring2_far(h, e):
        u, v = uv(h)
        all_of(wo.at[0, 0, 0:2], ring_s, far_r.at[h, e % 4]).wait_recv()
        d2d(h, place(h, u + e + 4, v + 2)).start()

    def in1():
        @pl.loop(1, 8)
        def _(i):
            p1(i, s1, r1, p1_s, p1_r).start()

        r1[zk] = s1[zk]

    def in1q():
        loads[3].wait()
        qt = q_ref[...].astype(f32).T.reshape(BLOCKS, CH, SPAN).astype(bf16).reshape(4, 16, 2, CH, SPAN)
        for i in range(8):
            s1q[i] = qt[i // 2, :, i % 2]

    def in1q_send():
        @pl.loop(1, 8)
        def _(i):
            p1(i, s1q, r1q, p1q_s, p1q_r).start()

        r1q[zk] = s1q[zk]

    def in2():
        all_of(r1.at[0:7], p1_s, p1_r).wait_recv()

        @pl.loop(1, 16)
        def _(i):
            p2(i, r1, r2, p2_s, p2_r).start()

        r2[xy] = r1[:, xy]

    def in2q():
        all_of(r1q.at[0:7], p1q_s, p1q_r).wait_recv()

        @pl.loop(1, 16)
        def _(i):
            p2(i, r1q, r2q, p2q_s, p2q_r).start()

        r2q[xy] = r1q[:, xy]

    def forward():
        all_of(r2.at[0:15], p2_s, p2_r).wait_recv()

        rows8[...] = r2[...].reshape(BLOCKS, 2 * CH, SPAN).astype(f32).reshape(BLOCKS * 2 * CH, SPAN)
        for r in range(2 * CH):
            part = rows8[pl.ds(r, BLOCKS, stride=2 * CH), :].astype(bf16)
            xcat[0:BLOCKS, r * SPAN : (r + 1) * SPAN] = part
            xcat[BLOCKS : 2 * BLOCKS, r * SPAN : (r + 1) * SPAN] = part
        for r in range(2 * CH):
            got = jnp.dot(t1_ref[...], xcat[:, r * SPAN : (r + 1) * SPAN], preferred_element_type=f32)
            re, im = got[:BLOCKS], got[BLOCKS:]
            hi, lo = split(jnp.concatenate([re * tw_ref[0] - im * tw_ref[1], re * tw_ref[1] + im * tw_ref[0]], 1))
            lhs2[r * BLOCKS : (r + 1) * BLOCKS, 0:256] = hi
            lhs2[r * BLOCKS : (r + 1) * BLOCKS, 256:512] = lo
            lhs2[r * BLOCKS : (r + 1) * BLOCKS, 512:768] = hi

    def middle():
        for c in range(CH):
            rows = pl.ds(c * BLOCKS, BLOCKS)
            left = jnp.dot(lhs2[rows, :], t2_ref[...], preferred_element_type=f32)
            right = jnp.dot(lhs2[pl.ds((c + CH) * BLOCKS, BLOCKS), :], t2_ref[...], preferred_element_type=f32)
            lr, li, rr, ri = left[:, :SPAN], left[:, SPAN:], right[:, :SPAN], right[:, SPAN:]
            hi, lo = split(jnp.concatenate([lr * rr - li * ri, lr * ri + li * rr], 1))
            lhs3[rows, 0:256] = hi
            lhs3[rows, 256:512] = lo
            lhs3[rows, 512:768] = hi
        for c in range(CH):
            rows = pl.ds(c * BLOCKS, BLOCKS)
            got = jnp.dot(lhs3[rows, :], t3_ref[...], preferred_element_type=f32)
            re, im = got[:, :SPAN], got[:, SPAN:]
            cols = pl.ds(c * SPAN, SPAN)
            hi, lo = split(jnp.concatenate([re * tw_ref[0] + im * tw_ref[1], im * tw_ref[0] - re * tw_ref[1]], 0))
            rhs4[0:256, cols] = hi
            rhs4[256:512, cols] = lo
            rhs4[512:768, cols] = hi

    def out1():
        all_of(r2q.at[0:15], p2q_s, p2q_r).wait_recv()

        rows4[...] = r2q[...].reshape(BLOCKS, CH, SPAN).astype(f32).reshape(BLOCKS * CH, SPAN)
        for c in range(CH):
            conv = jnp.dot(t4_ref[...], rhs4[:, c * SPAN : (c + 1) * SPAN], preferred_element_type=f32)
            at = pl.ds(c, BLOCKS, stride=CH)
            signal = rows8[pl.ds(c, BLOCKS, stride=2 * CH), :]
            rows4[at, :] = rows4[at, :] * (conv + skip_ref[0, me * CH + c] * signal)
        s3[...] = rows4[...].astype(bf16).reshape(16, 8, CH, SPAN)

        @pl.loop(1, 16)
        def _(i):
            p3(i).start()

        r3[xy] = s3[xy]

    def out2():
        all_of(r3.at[0:15], p3_s, p3_r).wait_recv()

        @pl.loop(1, 8)
        def _(i):
            p4(i, g).start()

        @pl.loop(0, 8)
        def _(i):
            p4(i, 1 - g).start()

        r4[g, z, :, k] = r3[:, zk]

    def project_here():
        all_of(r3.at[0:14], p4_s.at[g], p4_r.at[g]).wait_recv()

        own.wait()
        here = r4[g].reshape(512, SPAN).T

        @pl.loop(0, 16)
        def _(t):
            cols = pl.ds(pl.multiple_of(t * TILE, TILE), TILE)
            acc[:, cols] = jnp.dot(here, wown[:, cols], preferred_element_type=f32)

    def leave(i, base, size):
        cols = pl.ds(base, size)
        return pltpu.make_async_copy(result.at[:, cols], out_ref.at[:, cols], out_sem.at[i])

    leaving = [(t * TILE, TILE) for t in range(16)]

    def project_there():
        all_of(r3, p4_s.at[1 - g], p4_r.at[1 - g]).wait_recv()

        there = r4[1 - g].reshape(512, SPAN).T

        def finish(i, weight):
            base, size = leaving[i]
            total = acc[:, base : base + size] + jnp.dot(there, weight.reshape(512, size), preferred_element_type=f32)
            result[:, base : base + size] = total.astype(bf16)
            leave(i, base, size).start()

        for part in range(4):
            if part % 2 == 0:

                all_of(wo.at[0, :, 0:16], d2d_s, d2d_r.at[part // 2]).wait_recv()

            for t in range(4):
                finish(part * 4 + t, wo[part // 2, part % 2, :, :, t * TILE : (t + 1) * TILE])

    def sent():
        all_of(s1.at[0:7], p1_s, p1_r).wait_send()
        all_of(s1q.at[0:7], p1q_s, p1q_r).wait_send()
        all_of(r2.at[0:15], p2_s, p2_r).wait_send()
        all_of(r2q.at[0:15], p2q_s, p2q_r).wait_send()
        all_of(s3.at[0:15], p3_s, p3_r).wait_send()

        @pl.when(outer)
        def _():
            all_of(wo.at[0, 0, 0:8], fresh_s, seed_r.at[0, 0]).wait_send()


    @pl.when(outer)
    def _():
        for sub in (0, 1):
            for h in (0, 1):
                for far in (0, 1):
                    fresh(h, sub, far).start()

    in1()
    in1q()
    in1q_send()
    seed_step(0, 0)
    seed_step(1, 0)
    in2()
    seed_step(0, 1)
    in2q()
    seed_step(1, 1)
    forward()
    spread(0, 0)
    spread(1, 0)
    middle()
    out1()
    ring1(0)
    ring1(1)
    out2()
    for e in (0, -1, 1, 2):
        for h in (0, 1):
            ring2(h, e)
    project_here()
    sent()
    for e in (0, -1, 1, 2):
        for h in (0, 1):
            ring2_far(h, e)
    project_there()

    all_of(r3.at[0:14], p4_s.at[g], p4_r.at[g]).wait_send()
    all_of(r3, p4_s.at[1 - g], p4_r.at[1 - g]).wait_send()
    all_of(wo.at[:, :, 0:16], d2d_s, d2d_r.at[0]).wait_send()
    all_of(wo.at[:, :, 0:15], ring_s, st1_r.at[0]).wait_send()
    for i, (base, size) in enumerate(leaving):
        leave(i, base, size).wait()


def body(query_branch, key_branch, value_branch, filter_taps, skip_gain, out_weight):
    width = out_weight.shape[1]
    hbm = pl.BlockSpec(memory_space=pltpu.HBM)
    dma = pltpu.SemaphoreType.DMA
    v = pltpu.VMEM
    consts = tables()
    return pl.pallas_call(
        kernel,
        out_shape=jax.ShapeDtypeStruct((SPAN, width), bf16),
        in_specs=[hbm] * 4 + [pl.BlockSpec(memory_space=pltpu.SMEM)] + [hbm] * 6,
        out_specs=hbm,
        scratch_shapes=[
            v((SPAN, 512), bf16), v((SPAN, 512), bf16), v((SPAN, 512), bf16), v((SPAN, 512), f32),
            *[v(t.shape, t.dtype) for t in consts], dma((9,)),
            v((256, 256), bf16), v((768, 256), bf16), v((768, 256), bf16), v((128, 768), bf16),
            v((8, 16, 2 * CH, SPAN), bf16), v((8, 16, 2 * CH, SPAN), bf16), v((16, 8, 2 * CH, SPAN), bf16),
            v((8, 16, CH, SPAN), bf16), v((8, 16, CH, SPAN), bf16), v((16, 8, CH, SPAN), bf16),
            v((16, 8, CH, SPAN), bf16), v((16, 8, CH, SPAN), bf16), v((2, 4, 16, 2, CH, SPAN), bf16),
            v((512, width), bf16), v((2, 2, 32, 16, QUARTER), bf16), v((SPAN, width), f32),
            v((BLOCKS * 2 * CH, SPAN), f32), v((BLOCKS * CH, SPAN), f32),
            v((256, 2 * CH * SPAN), bf16), v((2 * CH * BLOCKS, 768), bf16), v((CH * BLOCKS, 768), bf16), v((768, CH * SPAN), bf16),
            dma, dma, dma, dma, dma, dma, dma, dma, dma, dma, dma, dma((2,)), dma((2,)),
            dma, dma, dma((2, 2)), dma((2,)), dma((2, 4)), dma((2, 4)), dma, dma((2,)), v((SPAN, width), bf16), dma((16,)),
        ],
        compiler_params=pltpu.CompilerParams(collective_id=0, has_side_effects=True, vmem_limit_bytes=56 * 2**20),
    )(query_branch, key_branch, value_branch, filter_taps, skip_gain.reshape(1, -1), *consts, out_weight)
def solution(mesh):
    return jax.shard_map(
        body,
        mesh=mesh,
        in_specs=(P("seq", "ch"), P("seq", "ch"), P("seq", "ch"), P("seq", "ch"), P("ch"), P("ch", None)),
        out_specs=P("seq", None),
        check_vma=False,
    )
```
